256 devices in a mesh: row: 2 (over core), cube: 128 (over y, x, z).
Axes of the slice: x: 4, y: 4, z: 8, core: 2. Of those that a mesh axis runs over, the one named last changes fastest.
Arguments:
- child_fronts: float32 [128, 96, 2, 3072], P('cube', None, 'row'), as said below
- root_front: float32 [128, 80, 2, 5120], P('cube', None, 'row'), as said below
- child_map: int32 [2, 23], replicated, may hold values from 0 to 39, as said below
Outputs:
- child_factor: float32 [128, 4, 2, 3072], P('cube', None, 'row')
- root_factor: float32 [128, 2, 2, 5120], P('cube', None, 'row')
- root_rest: float32 [128, 78, 2, 4992], P('cube', None, 'row')
The draws below stay inside these ranges and needn't reach their ends.
Inputs may be any that keep to these rules, and one draw needn't show every extreme that they name: `child_fronts`: each F_c is symmetric positive definite. `root_front`: A is symmetric positive definite. `child_map`: each row names 23 different blocks; both rows name block 0 and block 39.
All inputs are finite; a program needn't handle non-finite values.
Results may differ from the reference program's by a relative error of at most 0.0001.
Values sent between devices are 32-bit elements; how exact they have to be, the bound alone decides.
A program may use at most 128 MiB of HBM per device.

```python
import math
import jax
import jax.numpy as jnp
from jax import lax

CHILD_ORDER = 6144
ROOT_ORDER = 10240
BLOCK = 256
SUBCUBE = 64
CHILD_PIVOTS = 256
ROOT_PIVOTS = 256
UPDATE_BLOCKS = 23
ROOT_BLOCKS = 40
N_ROW = 2
N_CUBE = 128


def to_storage_drawn(matrix, members, halves):
    order_rows, order_cols = matrix.shape
    return jnp.transpose(matrix.reshape(order_rows // members, members, order_cols // halves, halves), (1, 0, 3, 2))


def symmetric_front(key, order, pivots, band_scale, wide_scale, lowest, highest, strength, base):
    first, second, third, fourth = jax.random.split(key, 4)
    near = jax.random.uniform(first, (order, order), jnp.float32, -1.0, 1.0)
    near = 0.5 * (near + near.T)
    farther = jax.random.uniform(second, (order, order), jnp.float32, -1.0, 1.0)
    farther = 0.5 * (farther + farther.T)
    rows_index = lax.broadcasted_iota(jnp.int32, (order, order), 0)
    cols_index = lax.broadcasted_iota(jnp.int32, (order, order), 1)
    distance = jnp.abs(rows_index - cols_index)
    offdiagonal = jnp.where(distance <= 2, band_scale * near, 0.0) + wide_scale / math.sqrt(order) * farther
    diagonal = jax.random.uniform(third, (order,), jnp.float32, lowest, highest)
    amplitude = math.sqrt(strength * 0.5 * (lowest + highest) / pivots)
    common = amplitude * (base + jax.random.uniform(fourth, (order,), jnp.float32, 0.0, 1.0))
    return jnp.where(distance == 0, diagonal[:, None], offdiagonal) + common[:, None] * common[None, :]


def front_law():
    return (0.1, 1.0, 1.6, 2.4, 3.0, 0.5)


def draw_child_fronts(key, part):
    key = jax.random.fold_in(key, 3)
    band_scale, wide_scale, lowest, highest, strength, base = front_law()
    stored = []
    for child_index in range(2):
        matrix = symmetric_front(jax.random.fold_in(key, child_index), CHILD_ORDER, CHILD_PIVOTS, band_scale, wide_scale, lowest, highest, strength, base)
        stored.append(to_storage_drawn(matrix, SUBCUBE, N_ROW))
    return jnp.concatenate(stored, 0)


def draw_root_front(key, part):
    key = jax.random.fold_in(key, 4)
    band_scale, wide_scale, lowest, highest, strength, base = front_law()
    matrix = symmetric_front(key, ROOT_ORDER, ROOT_PIVOTS, band_scale, wide_scale, lowest, highest, strength, base)
    return to_storage_drawn(matrix, N_CUBE, N_ROW)


def draw_child_map(key, part):
    key = jax.random.fold_in(key, 5)
    mappings = []
    for child_index in range(2):
        first, second = jax.random.split(jax.random.fold_in(key, child_index))
        inner = 1 + jax.random.permutation(first, ROOT_BLOCKS - 2)[:UPDATE_BLOCKS - 2]
        chosen = jnp.concatenate([jnp.array([0, ROOT_BLOCKS - 1], jnp.int32), inner.astype(jnp.int32)])
        mappings.append(jax.random.permutation(second, chosen))
    return jnp.stack(mappings).astype(jnp.int32)


def setup_inputs(seed: int = 0) -> dict:
    streams_of = jax.random.split(jax.random.key(seed), 4)
    child_fronts = draw_child_fronts(jax.random.fold_in(streams_of[3], 71), 0)
    root_front = draw_root_front(jax.random.fold_in(streams_of[3], 71), 0)
    child_map = draw_child_map(jax.random.fold_in(streams_of[3], 71), 0)
    return dict(child_fronts=child_fronts, root_front=root_front, child_map=child_map)


PRECISE = lax.Precision.HIGHEST

def to_logical(stored):
    members, slots, halves, columns = stored.shape
    return jnp.transpose(stored, (1, 0, 3, 2)).reshape(slots * members, columns * halves)

def to_storage(matrix, members, halves):
    order_rows, order_cols = matrix.shape
    return jnp.transpose(matrix.reshape(order_rows // members, members, order_cols // halves, halves), (1, 0, 3, 2))

def partial_factor(whole_front, pivots):
    lower_factor = jnp.linalg.cholesky(whole_front[:pivots, :pivots])
    factor = lax.linalg.triangular_solve(lower_factor, whole_front[:pivots], left_side=True, lower=True)
    coupling = factor[:, pivots:]
    schur_part = whole_front[pivots:, pivots:] - jnp.dot(coupling.T, coupling, precision=PRECISE)
    return (factor, schur_part)

def reference(child_fronts, root_front, child_map):
    assembled = to_logical(root_front)
    factors = []
    for child_index in range(2):
        child_front = to_logical(child_fronts[child_index * SUBCUBE:(child_index + 1) * SUBCUBE])
        factor, schur_part = partial_factor(child_front, CHILD_PIVOTS)
        factors.append(to_storage(factor, SUBCUBE, N_ROW))
        positions = (child_map[child_index][:, None] * BLOCK + jnp.arange(BLOCK, dtype=jnp.int32)[None, :]).reshape(-1)
        assembled = assembled.at[positions[:, None], positions[None, :]].add(schur_part)
    root_factor, root_schur = partial_factor(assembled, ROOT_PIVOTS)
    return (jnp.concatenate(factors, 0), to_storage(root_factor, N_CUBE, N_ROW), to_storage(root_schur, N_CUBE, N_ROW))
```

```python
import functools

import jax
import jax.numpy as jnp
from jax import lax
from jax.experimental import pallas as pl
from jax.experimental.pallas import tpu as pltpu
from jax.sharding import PartitionSpec as P

MESH = pl.DeviceIdType.MESH
LANES = 128
NX = 4
NZ = 8
PIVOTS = 256
UPDATE_BLOCKS = 23
ROOT_BLOCKS = 40
SUB = 64
GROUP = 8
PRECISE = lax.Precision.HIGHEST
VMEM_BYTES = 56 * 2**20
Z_ORDER = (0, 1, 7, 2, 6, 3, 5, 4)
RING = (1, 3, 2)


def dot(a, b, dims=(((1,), (0,)), ((), ()))):
    return lax.dot_general(a, b, dims, precision=PRECISE, preferred_element_type=jnp.float32)


def gather_kernel(slots, ny, cut, x_ref, out_ref, own_sem, z_send, z_recv, p_send, p_recv):
    me = lax.axis_index("cube")
    core = lax.axis_index("row")
    z = me % NZ
    x = me // NZ % NX
    y = me // (NZ * NX)
    ly = y % ny
    base = y - ly
    ring_y = RING if ny == 4 else (1,)

    def chip(py, px, pz):
        return (core, (base + py) * (NX * NZ) + px * NZ + pz)

    def over_x(d):
        return chip(ly, (x + d) % NX, z)

    def over_y(d):
        return chip((ly + d) % ny, x, z)

    def over_z(d):
        return chip(ly, x, (z + d) % NZ)

    barrier = pltpu.get_barrier_semaphore()
    peers = [over_z(d) for d in range(1, NZ)] + [over_x(d) for d in RING] + [over_y(d) for d in ring_y]
    for peer in peers:
        pl.semaphore_signal(barrier, inc=1, device_id=peer, device_id_type=MESH)
    pl.semaphore_wait(barrier, len(peers))

    first = pl.ds(0, cut)
    second = pl.ds(cut, slots - cut)
    started = []

    def send(src, dst, ssem, rsem, peer):
        copy = pltpu.make_async_remote_copy(
            src_ref=src, dst_ref=dst, send_sem=ssem, recv_sem=rsem, device_id=peer, device_id_type=MESH
        )
        copy.start()
        started.append(copy)
        return copy

    mine = pltpu.make_async_copy(x_ref, out_ref.at[:, ly, x, z], own_sem)
    mine.start()
    z_copies = {}
    for d in Z_ORDER[1:]:
        z_copies[d] = send(x_ref, out_ref.at[:, ly, x, z], z_send.at[d], z_recv.at[d], over_z(d))
    mine.wait()
    second_hop = []
    third_hop = []

    def third(t):
        zs = (z + NZ - Z_ORDER[t]) % NZ
        for copy in second_hop[t]:
            copy.wait_recv()
        for k, d in enumerate(ring_y):
            part = out_ref.at[first, ly, :, zs]
            third_hop.append(send(part, part, p_send.at[2, t, k], p_recv.at[2, t, k], over_y(d)))
        for k, d in enumerate(RING):
            part = out_ref.at[second, pl.ds(0, ny), x, zs]
            third_hop.append(send(part, part, p_send.at[3, t, k], p_recv.at[3, t, k], over_x(d)))

    for t, dz in enumerate(Z_ORDER):
        zs = (z + NZ - dz) % NZ
        if dz:
            z_copies[dz].wait_recv()
        hop = []
        for k, d in enumerate(RING):
            part = out_ref.at[first, ly, x, zs]
            hop.append(send(part, part, p_send.at[0, t, k], p_recv.at[0, t, k], over_x(d)))
        for k, d in enumerate(ring_y):
            part = out_ref.at[second, ly, x, zs]
            hop.append(send(part, part, p_send.at[1, t, k], p_recv.at[1, t, k], over_y(d)))
        second_hop.append(hop)
        if t >= 1:
            third(t - 1)
    third(NZ - 1)
    for copy in third_hop:
        copy.wait_recv()
    for copy in started:
        copy.wait_send()


def gather(rows, ny, cut, collective_id):
    slots, groups, lanes = rows.shape
    return pl.pallas_call(
        functools.partial(gather_kernel, slots, ny, cut),
        out_shape=jax.ShapeDtypeStruct((slots, ny, NX, NZ, groups, lanes), jnp.float32),
        in_specs=[pl.BlockSpec(memory_space=pl.ANY)],
        out_specs=pl.BlockSpec(memory_space=pl.ANY),
        scratch_shapes=[
            pltpu.SemaphoreType.DMA,
            pltpu.SemaphoreType.DMA((NZ,)),
            pltpu.SemaphoreType.DMA((NZ,)),
            pltpu.SemaphoreType.DMA((4, NZ, 3)),
            pltpu.SemaphoreType.DMA((4, NZ, 3)),
        ],
        compiler_params=pltpu.CompilerParams(
            collective_id=collective_id, has_side_effects=True, vmem_limit_bytes=VMEM_BYTES
        ),
        name="gather_pivot_rows",
    )(rows)


def interleave(parity):
    k = lax.broadcasted_iota(jnp.int32, (LANES, PIVOTS), 0)
    c = lax.broadcasted_iota(jnp.int32, (LANES, PIVOTS), 1)
    return (c == 2 * k + parity).astype(jnp.float32)


def sub_factor(block):
    rows = [block[i * GROUP : (i + 1) * GROUP] for i in range(SUB // GROUP)]
    sub = lax.broadcasted_iota(jnp.int32, (GROUP, LANES), 0)
    for g in range(SUB // GROUP):
        live = range(g, SUB // GROUP)
        cols = [
            {i: jnp.broadcast_to(rows[i][:, g * GROUP + k : g * GROUP + k + 1], (GROUP, LANES)) for i in live}
            for k in range(GROUP)
        ]
        scale = jnp.zeros((GROUP, LANES), jnp.float32)
        for j in range(GROUP):
            pivot = jnp.broadcast_to(cols[j][g][j : j + 1], (GROUP, LANES))
            inverse = 1.0 / pivot
            scale = jnp.where(sub == j, pivot, scale)
            line = jnp.broadcast_to(rows[g][j : j + 1], (GROUP, LANES))
            heads = {k: jnp.broadcast_to(cols[k][g][j : j + 1], (GROUP, LANES)) for k in range(j + 1, GROUP)}
            for i in live:
                factor = cols[j][i] * inverse
                if i == g:
                    factor = jnp.where(sub > j, factor, 0.0)
                for k in range(j + 1, GROUP):
                    cols[k][i] = cols[k][i] - factor * heads[k]
                rows[i] = rows[i] - factor * line
        root = lax.rsqrt(scale)
        root = root * (1.5 - 0.5 * scale * root * root)
        rows[g] = rows[g] * root
    return jnp.concatenate(rows, 0)[:, SUB:]


def cholesky_kernel(even_ref, odd_ref, inv_ref, d_ref):
    d_ref[...] = dot(even_ref[...], interleave(0)) + dot(odd_ref[...], interleave(1))
    r = lax.broadcasted_iota(jnp.int32, (PIVOTS, PIVOTS), 0)
    c = lax.broadcasted_iota(jnp.int32, (PIVOTS, PIVOTS), 1)
    inv_ref[...] = (r == c).astype(jnp.float32)
    rs = lax.broadcasted_iota(jnp.int32, (SUB, SUB), 0)
    cs = lax.broadcasted_iota(jnp.int32, (SUB, SUB), 1)
    eye = (rs == cs).astype(jnp.float32)
    for o in range(PIVOTS // SUB):
        lo, hi = o * SUB, (o + 1) * SUB
        tile = d_ref[lo:hi, lo:hi]
        small = sub_factor(jnp.concatenate([tile, eye], 1))
        done = dot(small, inv_ref[lo:hi, :])
        inv_ref[lo:hi, :] = done
        if hi < PIVOTS:
            lead = dot(small, d_ref[lo:hi, :])
            tail = lead[:, hi:]
            d_ref[hi:, :] = d_ref[hi:, :] - dot(tail, lead, (((0,), (0,)), ((), ())))
            inv_ref[hi:, :] = inv_ref[hi:, :] - dot(tail, done, (((0,), (0,)), ((), ())))


def inverse_factor(even, odd):
    return pl.pallas_call(
        cholesky_kernel,
        out_shape=jax.ShapeDtypeStruct((PIVOTS, PIVOTS), jnp.float32),
        scratch_shapes=[pltpu.VMEM((PIVOTS, PIVOTS), jnp.float32)],
        compiler_params=pltpu.CompilerParams(vmem_limit_bytes=VMEM_BYTES),
        name="inverse_factor",
    )(even, odd)


def solve_own(own_even, own_odd, inv):
    half = dot(own_even, dot(inv, interleave(0), (((1,), (1,)), ((), ()))), (((1,), (1,)), ((), ())))
    half = half + dot(own_odd, dot(inv, interleave(1), (((1,), (1,)), ((), ()))), (((1,), (1,)), ((), ())))
    return dot(half, inv)


def update_kernel(width, pivot_slots, members, front_ref, even_ref, odd_ref, inv_ref, pivots_ref, rest_ref, factor_ref, lhs):
    @pl.when(pl.program_id(0) == 0)
    def _():
        lhs[...] = solve_own(even_ref[...], odd_ref[...], inv_ref[...])

    p = lax.axis_index("cube") % members
    own = [inv_ref[pl.ds(i * members + p, 1), :] for i in range(pivot_slots)]
    pick = jnp.concatenate(own, 0)
    for k in range(width):
        part = pivots_ref[:, k, :]
        rest_ref[:, k, :] = front_ref[:, k, :] - dot(lhs[...], part)
        factor_ref[:, k, :] = dot(pick, part)


def update(front, even, odd, inv, pivots, pivot_slots, members):
    slots, groups, lanes = front.shape
    width = 8
    whole = lambda j: (0, 0)
    sliced = lambda j: (0, j, 0)
    return pl.pallas_call(
        functools.partial(update_kernel, width, pivot_slots, members),
        grid=(groups // width,),
        out_shape=(
            jax.ShapeDtypeStruct((slots, groups, lanes), jnp.float32),
            jax.ShapeDtypeStruct((pivot_slots, groups, lanes), jnp.float32),
        ),
        in_specs=[
            pl.BlockSpec((slots, width, lanes), sliced),
            pl.BlockSpec((slots, lanes), whole),
            pl.BlockSpec((slots, lanes), whole),
            pl.BlockSpec((PIVOTS, PIVOTS), whole),
            pl.BlockSpec((PIVOTS, width, lanes), sliced),
        ],
        out_specs=(
            pl.BlockSpec((slots, width, lanes), sliced),
            pl.BlockSpec((pivot_slots, width, lanes), sliced),
        ),
        scratch_shapes=[pltpu.VMEM((slots, PIVOTS), jnp.float32)],
        compiler_params=pltpu.CompilerParams(vmem_limit_bytes=VMEM_BYTES),
        name="update_rows",
    )(front, even, odd, inv, pivots)


def both_cores(block):
    parts = lax.all_gather(block, "row", axis=0, tiled=False)
    return parts[0], parts[1]


def eliminate(front, pivot_slots, ny, cut, collective_id):
    members = ny * NX * NZ
    pivots = gather(front[:pivot_slots], ny, cut, collective_id)
    pivots = pivots.reshape(PIVOTS, front.shape[1], LANES)
    even, odd = both_cores(pivots[:, 0, :])
    own_even, own_odd = both_cores(front[:, 0, :])
    inv = inverse_factor(even, odd)
    return update(front, own_even, own_odd, inv, pivots, pivot_slots, members)


def swapped(block):
    count = lax.axis_size("cube")
    return lax.ppermute(block, "cube", [(p, p ^ count // 2) for p in range(count)])


def place_blocks(pieces, mapping):
    targets = lax.broadcasted_iota(jnp.int32, (ROOT_BLOCKS, UPDATE_BLOCKS), 0)
    selector = (targets == mapping[None, :]).astype(jnp.float32)
    spread = jnp.einsum("mu,usvb->msvb", selector, pieces, precision=PRECISE)
    return jnp.einsum("nv,msvb->msnb", selector, spread, precision=PRECISE)


def shards(child_fronts, root_front, child_map):
    position = lax.axis_index("cube")
    half = lax.axis_size("cube") // 2
    child = child_fronts.reshape(child_fronts.shape[1], -1, LANES)
    root = root_front.reshape(root_front.shape[1], -1, LANES)
    child_rest, child_factor = eliminate(child, 4, 2, 2, 1)
    pieces = child_rest[4:, 1:].reshape(UPDATE_BLOCKS, 2, 2, UPDATE_BLOCKS, LANES)
    own_child = position // half
    staying = lax.dynamic_index_in_dim(pieces, own_child, 2, keepdims=False)
    leaving = lax.dynamic_index_in_dim(pieces, 1 - own_child, 2, keepdims=False)
    arrived = swapped(leaving)
    own_map = lax.dynamic_index_in_dim(child_map, own_child, 0, keepdims=False)
    other_map = lax.dynamic_index_in_dim(child_map, 1 - own_child, 0, keepdims=False)
    placed = place_blocks(staying, own_map) + place_blocks(arrived, other_map)
    assembled = root + placed.reshape(root.shape)
    root_rest, root_factor = eliminate(assembled, 2, 4, 1, 2)
    return (
        child_factor.reshape(1, 4, 1, -1),
        root_factor.reshape(1, 2, 1, -1),
        root_rest[2:, 1:].reshape(1, 78, 1, -1),
    )


def solution(mesh):
    placed = P("cube", None, "row", None)
    return jax.shard_map(
        shards, mesh=mesh, in_specs=(placed, placed, P()), out_specs=(placed, placed, placed), check_vma=False
    )
```

```python
import functools

import jax
import jax.numpy as jnp
from jax import lax
from jax.experimental import pallas as pl
from jax.experimental.pallas import tpu as pltpu
from jax.sharding import PartitionSpec as P

MESH = pl.DeviceIdType.MESH
LANES = 128
NX = 4
NZ = 8
PIVOTS = 256
UPDATE_BLOCKS = 23
ROOT_BLOCKS = 40
SUB = 64
GROUP = 8
PRECISE = lax.Precision.HIGHEST
VMEM_BYTES = 56 * 2**20
Z_ORDER = (0, 1, 7, 2, 6, 3, 5, 4)
RING = (1, 3, 2)
STRIDE = 3


def dot(a, b, dims=(((1,), (0,)), ((), ()))):
    return lax.dot_general(a, b, dims, precision=PRECISE, preferred_element_type=jnp.float32)


def gather_kernel(
    slots, ny, cut, x_ref, out_ref, inv_ref, own_ref, other_ref,
    d_ref, mine, theirs, diag, diag_other,
    local_sem, slab_sem, z_send, z_recv, p_send, p_recv, s_send, s_recv, t_send, t_recv,
):
    me = lax.axis_index("cube")
    core = lax.axis_index("row")
    z = me % NZ
    x = me // NZ % NX
    y = me // (NZ * NX)
    ly = y % ny
    base = y - ly
    ring_y = RING if ny == 4 else (1,)

    def chip(py, px, pz):
        return (core, (base + py) * (NX * NZ) + px * NZ + pz)

    def over_x(d):
        return chip(ly, (x + d) % NX, z)

    def over_y(d):
        return chip((ly + d) % ny, x, z)

    def over_z(d):
        return chip(ly, x, (z + d) % NZ)

    sibling = (1 - core, me)
    started = []

    def send(src, dst, ssem, rsem, peer):
        copy = pltpu.make_async_remote_copy(
            src_ref=src, dst_ref=dst, send_sem=ssem, recv_sem=rsem, device_id=peer, device_id_type=MESH
        )
        copy.start()
        started.append(copy)
        return copy

    head = x_ref.at[:, pl.ds(0, GROUP)]
    pivot_rows = x_ref.at[pl.ds(0, slots)]
    slab = pltpu.make_async_copy(head, mine, slab_sem)
    slab.start()
    local = pltpu.make_async_copy(pivot_rows, out_ref.at[:, ly, x, z], local_sem)
    local.start()

    barrier = pltpu.get_barrier_semaphore()
    peers = [over_z(d) for d in range(1, NZ)] + [over_x(d) for d in RING] + [over_y(d) for d in ring_y] + [sibling]
    for peer in peers:
        pl.semaphore_signal(barrier, inc=1, device_id=peer, device_id_type=MESH)
    slab.wait()
    diag[ly, x, z] = mine[0:slots, 0, :]
    pl.semaphore_wait(barrier, len(peers))

    def small(stage, k, part, peer):
        return send(part, part, t_send.at[stage, k], t_recv.at[stage, k], peer)

    small_z = [small(0, d, diag.at[ly, x, z], over_z(d)) for d in Z_ORDER[1:]]
    z_copies = {}
    for d in Z_ORDER[1:]:
        z_copies[d] = send(pivot_rows, out_ref.at[:, ly, x, z], z_send.at[d], z_recv.at[d], over_z(d))
    slabs = send(head, theirs, s_send.at[0], s_recv.at[0], sibling)
    local.wait()

    first = pl.ds(0, cut)
    second = pl.ds(cut, slots - cut)
    hops = {}
    thirds = {}
    last = []

    def z_slice(t):
        return (z + NZ - Z_ORDER[t]) % NZ

    def piece(kind, t, k, part, peer):
        return send(part, part, p_send.at[kind, t, k], p_recv.at[kind, t, k], peer)

    def hop(t):
        if t:
            z_copies[Z_ORDER[t]].wait_recv()
        zs = z_slice(t)
        hops[t] = [piece(0, t, k, out_ref.at[first, ly, x, zs], over_x(d)) for k, d in enumerate(RING)]
        hops[t] += [piece(1, t, k, out_ref.at[second, ly, x, zs], over_y(d)) for k, d in enumerate(ring_y)]

    def third(t):
        for copy in hops[t]:
            copy.wait_recv()
        zs = z_slice(t)
        ways = (1, 3) if ny == 4 else ring_y
        thirds[t] = (
            [piece(2, t, k, out_ref.at[first, ly, :, zs], over_y(d)) for k, d in enumerate(ways)],
            [piece(3, t, k, out_ref.at[second, pl.ds(0, ny), x, zs], over_x(d)) for k, d in enumerate((1, 3))],
        )

    def forward(t):
        zs = z_slice(t)
        over_ys, over_xs = thirds[t]
        if ny == 4:
            for k, d in enumerate((1, 3)):
                over_ys[k].wait_recv()
                part = out_ref.at[first, (ly + 4 - d) % 4, pl.ds(2 * k, 2), zs]
                last.append(piece(4, t, k, part, over_y(d)))
        else:
            last.extend(over_ys)
        for k, d in enumerate((1, 3)):
            over_xs[k].wait_recv()
            part = out_ref.at[second, pl.ds(k * (ny // 2), ny // 2), (x + 4 - d) % 4, zs]
            last.append(piece(5, t, k, part, over_x(d)))

    hop(0)
    for copy in small_z:
        copy.wait_recv()
    small_x = [small(1, d, diag.at[ly, x], over_x(d)) for d in RING]
    hop(1)
    hop(2)
    for copy in small_x:
        copy.wait_recv()
    small_y = [small(2, d, diag.at[ly], over_y(d)) for d in ring_y]
    hop(3)
    third(0)
    hop(4)
    third(1)
    for copy in small_y:
        copy.wait_recv()
    small_core = send(diag, diag_other, s_send.at[1], s_recv.at[1], sibling)
    hop(5)
    third(2)
    hop(6)
    third(3)
    slabs.wait_recv()
    own_ref[...] = mine[:, 0, :]
    other_ref[...] = theirs[:, 0, :]
    hop(7)
    small_core.wait_recv()
    d_ref[...] = dot(in_order(diag, slots), interleave(core)) + dot(in_order(diag_other, slots), interleave(1 - core))
    steps = factor_steps(d_ref, inv_ref)
    moves = [functools.partial(forward, 0), functools.partial(third, 4), functools.partial(forward, 1),
             functools.partial(third, 5), functools.partial(forward, 2), functools.partial(third, 6),
             functools.partial(forward, 3), functools.partial(third, 7), functools.partial(forward, 4),
             functools.partial(forward, 5), functools.partial(forward, 6), functools.partial(forward, 7)]
    count = 0
    for _ in steps:
        count += 1
        if count % STRIDE == 0 and moves:
            moves.pop(0)()
    for move in moves:
        move()
    for copy in last:
        copy.wait_recv()
    for copy in started:
        copy.wait_send()


def in_order(diag, slots):
    return jnp.concatenate([diag[:, :, :, i, :].reshape(-1, LANES) for i in range(slots)], 0)


def gather(front, slots, ny, cut, collective_id):
    rows, groups, lanes = front.shape
    anywhere = pl.BlockSpec(memory_space=pl.ANY)
    vmem = pl.BlockSpec(memory_space=pltpu.VMEM)
    diag = pltpu.VMEM((ny, NX, NZ, slots, lanes), jnp.float32)
    slab = pltpu.VMEM((rows, GROUP, lanes), jnp.float32)
    dma = pltpu.SemaphoreType.DMA
    return pl.pallas_call(
        functools.partial(gather_kernel, slots, ny, cut),
        out_shape=(
            jax.ShapeDtypeStruct((slots, ny, NX, NZ, groups, lanes), jnp.float32),
            jax.ShapeDtypeStruct((PIVOTS, PIVOTS), jnp.float32),
            jax.ShapeDtypeStruct((rows, lanes), jnp.float32),
            jax.ShapeDtypeStruct((rows, lanes), jnp.float32),
        ),
        in_specs=[anywhere],
        out_specs=(anywhere, vmem, vmem, vmem),
        scratch_shapes=[
            pltpu.VMEM((PIVOTS, PIVOTS), jnp.float32), slab, slab, diag, diag,
            dma, dma, dma((NZ,)), dma((NZ,)), dma((6, NZ, 3)), dma((6, NZ, 3)),
            dma((2,)), dma((2,)), dma((3, NZ)), dma((3, NZ)),
        ],
        compiler_params=pltpu.CompilerParams(
            collective_id=collective_id, has_side_effects=True, vmem_limit_bytes=VMEM_BYTES
        ),
        name="gather_pivot_rows",
    )(front)


def interleave(parity):
    k = lax.broadcasted_iota(jnp.int32, (LANES, PIVOTS), 0)
    c = lax.broadcasted_iota(jnp.int32, (LANES, PIVOTS), 1)
    return (c == 2 * k + parity).astype(jnp.float32)


def factor_steps(d_ref, inv_ref):
    r = lax.broadcasted_iota(jnp.int32, (PIVOTS, PIVOTS), 0)
    c = lax.broadcasted_iota(jnp.int32, (PIVOTS, PIVOTS), 1)
    inv_ref[...] = (r == c).astype(jnp.float32)
    rs = lax.broadcasted_iota(jnp.int32, (SUB, SUB), 0)
    cs = lax.broadcasted_iota(jnp.int32, (SUB, SUB), 1)
    eye = (rs == cs).astype(jnp.float32)
    sub = lax.broadcasted_iota(jnp.int32, (GROUP, LANES), 0)
    for o in range(PIVOTS // SUB):
        lo, hi = o * SUB, (o + 1) * SUB
        rest = jnp.concatenate([d_ref[lo:hi, lo:hi], eye], 1)
        done = []
        for g in range(SUB // GROUP):
            height = SUB - g * GROUP
            below = lax.broadcasted_iota(jnp.int32, (height, LANES), 0)
            cols = [
                jnp.broadcast_to(rest[:, g * GROUP + k : g * GROUP + k + 1], (height, LANES)) for k in range(GROUP)
            ]
            scale = jnp.zeros((GROUP, LANES), jnp.float32)
            for j in range(GROUP):
                pivot = cols[j][j : j + 1]
                scale = jnp.where(sub == j, jnp.broadcast_to(pivot, (GROUP, LANES)), scale)
                factor = cols[j] * jnp.broadcast_to(1.0 / pivot, (height, LANES))
                factor = jnp.where(below > j, factor, 0.0)
                for k in range(j + 1, GROUP):
                    cols[k] = cols[k] - factor * jnp.broadcast_to(cols[k][j : j + 1], (height, LANES))
                rest = rest - factor * jnp.broadcast_to(rest[j : j + 1], (height, LANES))
            root = lax.rsqrt(scale)
            root = root * (1.5 - 0.5 * scale * root * root)
            done.append(rest[:GROUP] * root)
            rest = rest[GROUP:]
            yield
        small = jnp.concatenate(done, 0)[:, SUB:]
        top = dot(small, inv_ref[lo:hi, :])
        inv_ref[lo:hi, :] = top
        if hi < PIVOTS:
            lead = dot(small, d_ref[lo:hi, :])
            tail = lead[:, hi:]
            d_ref[hi:, :] = d_ref[hi:, :] - dot(tail, lead, (((0,), (0,)), ((), ())))
            inv_ref[hi:, :] = inv_ref[hi:, :] - dot(tail, top, (((0,), (0,)), ((), ())))
        yield


def solve_own(own, other, inv, core):
    across = (((1,), (1,)), ((), ()))
    half = dot(own, dot(inv, interleave(core), across), across)
    half = half + dot(other, dot(inv, interleave(1 - core), across), across)
    return dot(half, inv)


def split(a):
    high = a.astype(jnp.bfloat16)
    return high, (a - high.astype(jnp.float32)).astype(jnp.bfloat16)


def update_kernel(pivot_slots, members, compact, front_ref, own_ref, other_ref, inv_ref, pivots_ref, rest_ref, factor_ref, high_ref, low_ref):
    slots = front_ref.shape[0]
    step = pl.program_id(0)

    @pl.when(step == 0)
    def _():
        core = lax.axis_index("row")
        p = lax.axis_index("cube") % members
        rows = [solve_own(own_ref[...], other_ref[...], inv_ref[...], core)]
        rows += [inv_ref[pl.ds(i * members + p, 1), :] for i in range(pivot_slots)]
        rows += [jnp.zeros((high_ref.shape[0] - slots - pivot_slots, PIVOTS), jnp.float32)]
        high_ref[...], low_ref[...] = split(jnp.concatenate(rows, 0))

    product = functools.partial(jnp.dot, preferred_element_type=jnp.float32)
    for k in range(0, GROUP, 2):
        high, low = split(jnp.concatenate([pivots_ref[:, k, :], pivots_ref[:, k + 1, :]], 1))
        total = product(high_ref[...], high) + (product(high_ref[...], low) + product(low_ref[...], high))
        for e in range(2):
            part = total[:, e * LANES : (e + 1) * LANES]
            rest = front_ref[:, k + e, :] - part[:slots]
            factor_ref[:, k + e, :] = part[slots : slots + pivot_slots]
            if not compact:
                rest_ref[:, k + e, :] = rest
            elif k + e:
                rest_ref[pl.ds(step * GROUP + k + e - 1, slots - pivot_slots, compact), :] = rest[pivot_slots:]
            else:

                @pl.when(step > 0)
                def _():
                    rest_ref[pl.ds(step * GROUP - 1, slots - pivot_slots, compact), :] = rest[pivot_slots:]


def update(front, own, other, inv, pivots, pivot_slots, members, compact):
    slots, groups, lanes = front.shape
    height = -(-(slots + pivot_slots) // 16) * 16
    whole = lambda j: (0, 0)
    sliced = lambda j: (0, j, 0)
    if compact:
        rest_shape = ((slots - pivot_slots) * compact, lanes)
        rest_spec = pl.BlockSpec(rest_shape, whole)
    else:
        rest_shape = (slots, groups, lanes)
        rest_spec = pl.BlockSpec((slots, GROUP, lanes), sliced)
    return pl.pallas_call(
        functools.partial(update_kernel, pivot_slots, members, compact),
        grid=(groups // GROUP,),
        out_shape=(
            jax.ShapeDtypeStruct(rest_shape, jnp.float32),
            jax.ShapeDtypeStruct((pivot_slots, groups, lanes), jnp.float32),
        ),
        in_specs=[
            pl.BlockSpec((slots, GROUP, lanes), sliced),
            pl.BlockSpec((slots, lanes), whole),
            pl.BlockSpec((slots, lanes), whole),
            pl.BlockSpec((PIVOTS, PIVOTS), whole),
            pl.BlockSpec((PIVOTS, GROUP, lanes), sliced),
        ],
        out_specs=(rest_spec, pl.BlockSpec((pivot_slots, GROUP, lanes), sliced)),
        scratch_shapes=[pltpu.VMEM((height, PIVOTS), jnp.bfloat16), pltpu.VMEM((height, PIVOTS), jnp.bfloat16)],
        compiler_params=pltpu.CompilerParams(vmem_limit_bytes=VMEM_BYTES),
        name="update_rows",
    )(front, own, other, inv, pivots)


def eliminate(front, pivot_slots, ny, cut, collective_id, compact):
    members = ny * NX * NZ
    pivots, inv, own, other = gather(front, pivot_slots, ny, cut, collective_id)
    pivots = pivots.reshape(PIVOTS, front.shape[1], LANES)
    return update(front, own, other, inv, pivots, pivot_slots, members, compact)


def swapped(block):
    count = lax.axis_size("cube")
    return lax.ppermute(block, "cube", [(p, p ^ count // 2) for p in range(count)])


def place_blocks(pieces, mapping):
    targets = lax.broadcasted_iota(jnp.int32, (ROOT_BLOCKS, UPDATE_BLOCKS), 0)
    selector = (targets == mapping[None, :]).astype(jnp.float32)
    spread = jnp.einsum("mu,usvb->msvb", selector, pieces, precision=PRECISE)
    return jnp.einsum("nv,msvb->msnb", selector, spread, precision=PRECISE)


def shards(child_fronts, root_front, child_map):
    position = lax.axis_index("cube")
    half = lax.axis_size("cube") // 2
    child = child_fronts.reshape(child_fronts.shape[1], -1, LANES)
    root = root_front.reshape(root_front.shape[1], -1, LANES)
    child_rest, child_factor = eliminate(child, 4, 2, 2, 1, 0)
    pieces = child_rest[4:, 1:].reshape(UPDATE_BLOCKS, 2, 2, UPDATE_BLOCKS, LANES)
    own_child = position // half
    staying = lax.dynamic_index_in_dim(pieces, own_child, 2, keepdims=False)
    leaving = lax.dynamic_index_in_dim(pieces, 1 - own_child, 2, keepdims=False)
    arrived = swapped(leaving)
    own_map = lax.dynamic_index_in_dim(child_map, own_child, 0, keepdims=False)
    other_map = lax.dynamic_index_in_dim(child_map, 1 - own_child, 0, keepdims=False)
    placed = place_blocks(staying, own_map) + place_blocks(arrived, other_map)
    assembled = root + placed.reshape(root.shape)
    root_rest, root_factor = eliminate(assembled, 2, 4, 1, 2, ROOT_BLOCKS - 1)
    return (
        child_factor.reshape(1, 4, 1, -1),
        root_factor.reshape(1, 2, 1, -1),
        root_rest.reshape(1, 78, 1, -1),
    )


def solution(mesh):
    placed = P("cube", None, "row", None)
    return jax.shard_map(
        shards, mesh=mesh, in_specs=(placed, placed, P()), out_specs=(placed, placed, placed), check_vma=False
    )
```

```python
import functools

import jax
import jax.numpy as jnp
from jax import lax
from jax.experimental import pallas as pl
from jax.experimental.pallas import tpu as pltpu
from jax.sharding import PartitionSpec as P

MESH = pl.DeviceIdType.MESH
LANES = 128
NX = 4
NZ = 8
PIVOTS = 256
UPDATE_BLOCKS = 23
ROOT_BLOCKS = 40
PIECE_ROWS = 48
SUB = 64
GROUP = 8
PRECISE = lax.Precision.HIGHEST
VMEM_BYTES = 56 * 2**20
Z_ORDER = (0, 1, 7, 2, 6, 3, 5, 4)
RING = (1, 3, 2)


def dot(a, b, dims=(((1,), (0,)), ((), ()))):
    return lax.dot_general(a, b, dims, precision=PRECISE, preferred_element_type=jnp.float32)


def interleave(parity):
    k = lax.broadcasted_iota(jnp.int32, (LANES, PIVOTS), 0)
    c = lax.broadcasted_iota(jnp.int32, (LANES, PIVOTS), 1)
    return (c == 2 * k + parity).astype(jnp.float32)


def factor_steps(d_ref, inv_ref):
    r = lax.broadcasted_iota(jnp.int32, (PIVOTS, PIVOTS), 0)
    c = lax.broadcasted_iota(jnp.int32, (PIVOTS, PIVOTS), 1)
    inv_ref[...] = (r == c).astype(jnp.float32)
    rs = lax.broadcasted_iota(jnp.int32, (SUB, SUB), 0)
    cs = lax.broadcasted_iota(jnp.int32, (SUB, SUB), 1)
    eye = (rs == cs).astype(jnp.float32)
    sub = lax.broadcasted_iota(jnp.int32, (GROUP, LANES), 0)
    for o in range(PIVOTS // SUB):
        lo, hi = o * SUB, (o + 1) * SUB
        rest = jnp.concatenate([d_ref[lo:hi, lo:hi], eye], 1)
        done = []
        for g in range(SUB // GROUP):
            height = SUB - g * GROUP
            below = lax.broadcasted_iota(jnp.int32, (height, LANES), 0)
            cols = [
                jnp.broadcast_to(rest[:, g * GROUP + k : g * GROUP + k + 1], (height, LANES)) for k in range(GROUP)
            ]
            scale = jnp.zeros((GROUP, LANES), jnp.float32)
            for j in range(GROUP):
                pivot = cols[j][j : j + 1]
                scale = jnp.where(sub == j, jnp.broadcast_to(pivot, (GROUP, LANES)), scale)
                factor = cols[j] * jnp.broadcast_to(1.0 / pivot, (height, LANES))
                factor = jnp.where(below > j, factor, 0.0)
                for k in range(j + 1, GROUP):
                    cols[k] = cols[k] - factor * jnp.broadcast_to(cols[k][j : j + 1], (height, LANES))
                rest = rest - factor * jnp.broadcast_to(rest[j : j + 1], (height, LANES))
            root = lax.rsqrt(scale)
            root = root * (1.5 - 0.5 * scale * root * root)
            done.append(rest[:GROUP] * root)
            rest = rest[GROUP:]
            yield
        small = jnp.concatenate(done, 0)[:, SUB:]
        top = dot(small, inv_ref[lo:hi, :])
        inv_ref[lo:hi, :] = top
        if hi < PIVOTS:
            lead = dot(small, d_ref[lo:hi, :])
            tail = lead[:, hi:]
            d_ref[hi:, :] = d_ref[hi:, :] - dot(tail, lead, (((0,), (0,)), ((), ())))
            inv_ref[hi:, :] = inv_ref[hi:, :] - dot(tail, top, (((0,), (0,)), ((), ())))
        yield


class Torus:
    def __init__(self, ny):
        self.me = lax.axis_index("cube")
        self.core = lax.axis_index("row")
        self.ny = ny
        self.z = self.me % NZ
        self.x = self.me // NZ % NX
        self.y = self.me // (NZ * NX)
        self.ly = self.y % ny
        self.base = self.y - self.ly
        self.ring_y = RING if ny == 4 else (1,)
        self.sibling = (1 - self.core, self.me)
        half = lax.axis_size("cube") // 2
        self.across = (self.core, (self.me + half) % (2 * half))
        self.started = []

    def chip(self, py, px, pz):
        return (self.core, (self.base + py) * (NX * NZ) + px * NZ + pz)

    def over_x(self, d):
        return self.chip(self.ly, (self.x + d) % NX, self.z)

    def over_y(self, d):
        return self.chip((self.ly + d) % self.ny, self.x, self.z)

    def over_z(self, d):
        return self.chip(self.ly, self.x, (self.z + d) % NZ)

    def peers(self):
        columns = [self.chip(self.ly, self.x, (self.z + d) % NZ) for d in range(1, NZ)]
        found = columns + [self.sibling]
        found += [self.over_x(d) for d in RING]
        return found + [(self.core, (self.y + d) % 4 * (NX * NZ) + self.x * NZ + self.z) for d in RING]

    def send(self, src, dst, ssem, rsem, peer):
        copy = pltpu.make_async_remote_copy(
            src_ref=src, dst_ref=dst, send_sem=ssem, recv_sem=rsem, device_id=peer, device_id_type=MESH
        )
        copy.start()
        self.started.append(copy)
        return copy


def gather_and_factor(at, first, second, pivots, inv_ref, d_ref, mine, theirs, diag, sems, meanwhile):
    z_send, z_recv, p_send, p_recv, s_send, s_recv, t_send, t_recv = sems
    ny, x, z, ly = at.ny, at.x, at.z, at.ly
    over_x, over_y, over_z = at.over_x, at.over_y, at.over_z

    def small(stage, k, part, peer):
        return at.send(part, part, t_send.at[stage, k], t_recv.at[stage, k], peer)

    own = pivots.at[:, ly, x, z]
    tile = diag.at[at.core, ly, x, z]
    small_z = [small(0, d, tile, over_z(d)) for d in Z_ORDER[1:]]
    z_copies = {d: at.send(own, own, z_send.at[d], z_recv.at[d], over_z(d)) for d in Z_ORDER[1:]}
    blocks = at.send(mine, theirs, s_send, s_recv, at.sibling)
    hops = {}
    thirds = {}
    last = []

    def z_slice(t):
        return (z + NZ - Z_ORDER[t]) % NZ

    def view(part, py, px, t):
        return pivots.at[part[0], py, px, z_slice(t), part[1]]

    def piece(kind, t, k, part, peer):
        return at.send(part, part, p_send.at[kind, t, k], p_recv.at[kind, t, k], peer)

    def hop(t):
        if t:
            z_copies[Z_ORDER[t]].wait_recv()
        hops[t] = [piece(0, t, k, view(first, ly, x, t), over_x(d)) for k, d in enumerate(RING)]
        hops[t] += [piece(1, t, k, view(second, ly, x, t), over_y(d)) for k, d in enumerate(at.ring_y)]

    def third(t):
        for copy in hops[t]:
            copy.wait_recv()
        ways = (1, 3) if ny == 4 else at.ring_y
        thirds[t] = (
            [piece(2, t, k, view(first, ly, pl.ds(0, NX), t), over_y(d)) for k, d in enumerate(ways)],
            [piece(3, t, k, view(second, pl.ds(0, ny), x, t), over_x(d)) for k, d in enumerate((1, 3))],
        )

    def forward(t):
        over_ys, over_xs = thirds[t]
        if ny == 4:
            for k, d in enumerate((1, 3)):
                over_ys[k].wait_recv()
                last.append(piece(4, t, k, view(first, (ly + 4 - d) % 4, pl.ds(2 * k, 2), t), over_y(d)))
        else:
            last.extend(over_ys)
        for k, d in enumerate((1, 3)):
            over_xs[k].wait_recv()
            part = view(second, pl.ds(k * (ny // 2), ny // 2), (x + 4 - d) % 4, t)
            last.append(piece(5, t, k, part, over_x(d)))

    for copy in small_z:
        copy.wait_recv()
    small_x = [small(1, d, diag.at[at.core, ly, x], over_x(d)) for d in RING]
    hop(0)
    hop(1)
    hop(2)
    hop(3)
    hop(4)
    for copy in small_x:
        copy.wait_recv()
    small_y = [small(2, d, diag.at[at.core, ly], over_y(d)) for d in at.ring_y]
    hop(5)
    third(0)
    hop(6)
    third(1)
    third(2)
    hop(7)
    third(3)
    third(4)
    for copy in small_y:
        copy.wait_recv()
    small_core = small(3, 0, diag.at[at.core], at.sibling)
    meanwhile()
    small_core.wait_recv()
    d_ref[...] = dot(in_order(diag, 0), interleave(0)) + dot(in_order(diag, 1), interleave(1))
    moves = {0: ((third, 5), (forward, 0),), 3: ((third, 6), (forward, 1),), 6: ((third, 7), (forward, 2),), 10: ((forward, 3),), 15: ((forward, 4),), 20: ((forward, 5),), 25: ((forward, 6),), 30: ((forward, 7),)}
    for count, _ in enumerate(factor_steps(d_ref, inv_ref)):
        for move, t in moves.pop(count, ()):
            move(t)
    blocks.wait_recv()
    for group in moves.values():
        for move, t in group:
            move(t)

    def finish():
        for copy in last:
            copy.wait_recv()

    return finish


def in_order(diag, core):
    return jnp.concatenate([diag[core, :, :, :, i, :].reshape(-1, LANES) for i in range(diag.shape[4])], 0)


def solve_own(own, other, inv, core):
    across = (((1,), (1,)), ((), ()))
    half = dot(own, dot(inv, interleave(core), across), across)
    half = half + dot(other, dot(inv, interleave(1 - core), across), across)
    return dot(half, inv)


def split(a):
    high = a.astype(jnp.bfloat16)
    return high, (a - high.astype(jnp.float32)).astype(jnp.bfloat16)


def product(left, right):
    mul = functools.partial(jnp.dot, preferred_element_type=jnp.float32)
    (high, low), (top, rest) = left, right
    return mul(high, top) + (mul(high, rest) + mul(low, top))


def left_side(at, slots, pivot_slots, inv_ref, mine, theirs, sides, high_ref, low_ref):
    members = at.ny * NX * NZ
    inv = inv_ref[...]
    top = [-solve_own(mine[...], theirs[...], inv, at.core)] + sides
    rows = [inv_ref[pl.ds(i * members + at.me % members, 1), :] for i in range(pivot_slots)]
    rows += [jnp.zeros((high_ref.shape[0] - slots - pivot_slots, PIVOTS), jnp.float32)]
    below = jnp.concatenate(rows, 0)
    if sides:
        wide = sum(side.shape[1] for side in sides)
        below = jnp.concatenate([below, jnp.zeros((below.shape[0], wide), jnp.float32)], 1)
        top = [jnp.concatenate(top, 1)]
    high_ref[...], low_ref[...] = split(jnp.concatenate(top + [below], 0))


def along_lanes(map_ref, child, shape, per):
    lane = lax.broadcasted_iota(jnp.int32, shape, 1)
    found = jnp.full(shape, -1, jnp.int32)
    for u in range(UPDATE_BLOCKS):
        inside = lane == u + 1 if per == 1 else (lane == 2 * u) | (lane == 2 * u + 1)
        found = jnp.where(inside, map_ref[child, u], found)
    return found


def column_selector(map_ref, child):
    shape = (ROOT_BLOCKS, UPDATE_BLOCKS + 1)
    return (lax.broadcasted_iota(jnp.int32, shape, 0) == along_lanes(map_ref, child, shape, 1)).astype(jnp.float32)


def row_selector(map_ref, child):
    shape = (2 * ROOT_BLOCKS, PIECE_ROWS)
    row = lax.broadcasted_iota(jnp.int32, shape, 0)
    lane = lax.broadcasted_iota(jnp.int32, shape, 1)
    found = along_lanes(map_ref, child, shape, 2)
    return ((found >= 0) & (row == 2 * found + (lane & 1))).astype(jnp.float32)


def kernel(
    place_ref, map_ref, child_ref, root_ref, rest_ref, root_factor_ref, child_factor_ref,
    inv_ref, d_ref, few_own, few_other, held, leave, other, update,
    c_front, c_pivots, c_mine, c_theirs, c_diag, c_high, c_low,
    r_front, r_pivots, r_mine, r_theirs, r_diag, r_high, r_low,
    local_sem, *sems,
):
    c_sems, r_sems, (x_send, x_recv) = sems[:8], sems[8:16], sems[16:]
    at = Torus(2)
    slots, groups = child_ref.shape[0], child_ref.shape[1]
    pivot_slots = child_factor_ref.shape[0]
    whole = pltpu.make_async_copy(child_ref, c_front, local_sem.at[0])
    whole.start()
    local = pltpu.make_async_copy(child_ref.at[pl.ds(0, pivot_slots)], c_pivots.at[:, at.ly, at.x, at.z], local_sem.at[1])
    local.start()
    barrier = pltpu.get_barrier_semaphore()
    peers = at.peers()
    for peer in peers:
        pl.semaphore_signal(barrier, inc=1, device_id=peer, device_id_type=MESH)
    root_whole = pltpu.make_async_copy(root_ref, r_front, local_sem.at[2])
    root_whole.start()
    own_child = at.me // (lax.axis_size("cube") // 2)
    nothing = jnp.zeros((PIECE_ROWS, LANES), jnp.float32)
    held[0] = nothing
    leave[0] = nothing
    row_own, row_other = row_selector(map_ref, own_child), row_selector(map_ref, 1 - own_child)
    col_own, col_other = column_selector(map_ref, own_child), column_selector(map_ref, 1 - own_child)
    whole.wait()
    c_mine[...] = c_front[:, 0, :]
    c_diag[at.core, at.ly, at.x, at.z] = c_front[0:pivot_slots, 0, :]
    local.wait()
    pl.semaphore_wait(barrier, len(peers))

    all_groups = pl.ds(0, groups)
    halves = ((pl.ds(0, 2), all_groups), (pl.ds(2, 2), all_groups))
    finish = gather_and_factor(at, *halves, c_pivots, inv_ref, d_ref, c_mine, c_theirs, c_diag, c_sems, lambda: None)
    left_side(at, slots, pivot_slots, inv_ref, c_mine, c_theirs, [], c_high, c_low)
    left = (c_high[...], c_low[...])
    finish()
    count = (slots - pivot_slots) // 2
    fill = nothing[: PIECE_ROWS - count]
    for k in range(0, groups, 2):
        pair = [c_pivots[:, :, :, :, k + e, :].reshape(PIVOTS, LANES) for e in range(2)]
        total = product(left, split(jnp.concatenate(pair, 1)))
        for e in range(2):
            part = total[:, e * LANES : (e + 1) * LANES]
            child_factor_ref[:, k + e, :] = part[slots : slots + pivot_slots]
            if k + e:
                update[k + e] = c_front[:, k + e, :] + part[:slots]
                even = update[k + e, pl.ds(pivot_slots, count, 2), :]
                odd = update[k + e, pl.ds(pivot_slots + 1, count, 2), :]
                held[k + e] = jnp.concatenate([jnp.where(own_child == 0, even, odd), fill], 0)
                leave[k + e] = jnp.concatenate([jnp.where(own_child == 0, odd, even), fill], 0)

    sent = at.started
    at = Torus(4)
    lead = jnp.maximum(place_ref[own_child, 0], 1)
    blocks = UPDATE_BLOCKS + 1
    for s in range(2):
        few_own[s, 0:blocks] = leave[:, pl.ds(2 * lead - 2 + s, 1), :].reshape(blocks, LANES)
    few_own[2] = leave[lead]
    few = at.send(few_own, few_other, x_send.at[0], x_recv.at[0], at.across)
    root_whole.wait()
    slots, groups = root_ref.shape[0], root_ref.shape[1]
    pivot_slots = root_factor_ref.shape[0]
    lines = []
    for s in range(pivot_slots):
        line = held[:, pl.ds(2 * lead - 2 + s, 1), :].reshape(blocks, LANES)
        lines.append(r_front[s, :, :] + dot(col_own, line))
    column = r_front[:, 0, :] + dot(row_own, held[lead])
    few.wait_recv()
    for s in range(pivot_slots):
        line = lines[s] + dot(col_other, few_other[s, 0:blocks])
        r_pivots[s, at.ly, at.x, at.z] = line
        r_diag[at.core, at.ly, at.x, at.z, s : s + 1, :] = line[0:1]
    r_mine[...] = column + dot(row_other, few_other[2])
    bulk = []

    def exchange():
        bulk.append(at.send(leave, other, x_send.at[1], x_recv.at[1], at.across))

    all_slots = pl.ds(0, pivot_slots)
    halves = ((all_slots, pl.ds(0, 16)), (all_slots, pl.ds(16, groups - 16)))
    finish = gather_and_factor(at, *halves, r_pivots, inv_ref, d_ref, r_mine, r_theirs, r_diag, r_sems, exchange)
    left_side(at, slots, pivot_slots, inv_ref, r_mine, r_theirs, [row_own, row_other], r_high, r_low)
    left = (r_high[...], r_low[...])
    bulk[0].wait_recv()
    finish()
    for k in range(0, groups, 2):
        pair = []
        for n in (k, k + 1):
            pivots = r_pivots[:, :, :, :, n, :].reshape(PIVOTS, LANES)
            kept, arrived = held[place_ref[own_child, n]], other[place_ref[1 - own_child, n]]
            pair.append(jnp.concatenate([pivots, kept, arrived], 0))
        total = product(left, split(jnp.concatenate(pair, 1)))
        for e in range(2):
            part = total[:, e * LANES : (e + 1) * LANES]
            root_factor_ref[:, k + e, :] = part[slots : slots + pivot_slots]
            if k + e:
                rest = r_front[:, k + e, :] + part[:slots]
                rest_ref[pl.ds(k + e - 1, slots - pivot_slots, groups - 1), :] = rest[pivot_slots:]
    for copy in sent + at.started:
        copy.wait_send()


def buffers(front, slots, ny, depth):
    rows, groups, lanes = front.shape
    f32 = jnp.float32
    height = -(-(rows + slots) // 16) * 16
    return [
        pltpu.VMEM((rows, groups, lanes), f32),
        pltpu.VMEM((slots, ny, NX, NZ, groups, lanes), f32),
        pltpu.VMEM((rows, lanes), f32),
        pltpu.VMEM((rows, lanes), f32),
        pltpu.VMEM((2, ny, NX, NZ, slots, lanes), f32),
        pltpu.VMEM((height, depth), jnp.bfloat16),
        pltpu.VMEM((height, depth), jnp.bfloat16),
    ]


def semaphores():
    dma = pltpu.SemaphoreType.DMA
    return [dma((NZ,)), dma((NZ,)), dma((6, NZ, 3)), dma((6, NZ, 3)), dma, dma, dma((4, NZ)), dma((4, NZ))]


def eliminate(place, child_map, child, root):
    f32 = jnp.float32
    lanes = LANES
    dma = pltpu.SemaphoreType.DMA
    anywhere = pl.BlockSpec(memory_space=pl.ANY)
    in_vmem = pl.BlockSpec(memory_space=pltpu.VMEM)
    in_smem = pl.BlockSpec(memory_space=pltpu.SMEM)
    child_slots, root_slots = 4, 2
    few = pltpu.VMEM((3, PIECE_ROWS, lanes), f32)
    piece = pltpu.VMEM((UPDATE_BLOCKS + 1, PIECE_ROWS, lanes), f32)
    return pl.pallas_call(
        kernel,
        out_shape=(
            jax.ShapeDtypeStruct(((root.shape[0] - root_slots) * (root.shape[1] - 1), lanes), f32),
            jax.ShapeDtypeStruct((root_slots, root.shape[1], lanes), f32),
            jax.ShapeDtypeStruct((child_slots, child.shape[1], lanes), f32),
        ),
        in_specs=[in_smem, in_smem, anywhere, anywhere],
        out_specs=(in_vmem, in_vmem, in_vmem),
        scratch_shapes=[
            pltpu.VMEM((PIVOTS, PIVOTS), f32), pltpu.VMEM((PIVOTS, PIVOTS), f32), few, few, piece, piece, piece,
            pltpu.VMEM((child.shape[1], child.shape[0], lanes), f32),
            *buffers(child, child_slots, 2, PIVOTS), *buffers(root, root_slots, 4, PIVOTS + 2 * PIECE_ROWS),
            dma((3,)), *semaphores(), *semaphores(), dma((2,)), dma((2,)),
        ],
        compiler_params=pltpu.CompilerParams(
            collective_id=1, has_side_effects=True, vmem_limit_bytes=VMEM_BYTES
        ),
        name="eliminate_fronts",
    )(place, child_map, child, root)


def shards(child_fronts, root_front, child_map):
    child = child_fronts.reshape(child_fronts.shape[1], -1, LANES)
    root = root_front.reshape(root_front.shape[1], -1, LANES)
    blocks = jnp.arange(ROOT_BLOCKS, dtype=jnp.int32)[None, :, None]
    order = jnp.arange(1, UPDATE_BLOCKS + 1, dtype=jnp.int32)
    place = jnp.max(jnp.where(blocks == child_map[:, None, :], order, 0), 2)
    root_rest, root_factor, child_factor = eliminate(place, child_map, child, root)
    return (
        child_factor.reshape(1, 4, 1, -1),
        root_factor.reshape(1, 2, 1, -1),
        root_rest.reshape(1, 78, 1, -1),
    )


def solution(mesh):
    placed = P("cube", None, "row", None)
    return jax.shard_map(
        shards, mesh=mesh, in_specs=(placed, placed, P()), out_specs=(placed, placed, placed), check_vma=False
    )
```

```python
import functools

import jax
import jax.numpy as jnp
from jax import lax
from jax.experimental import pallas as pl
from jax.experimental.pallas import tpu as pltpu
from jax.sharding import PartitionSpec as P

MESH = pl.DeviceIdType.MESH
LANES = 128
NX = 4
NZ = 8
PIVOTS = 256
UPDATE_BLOCKS = 23
ROOT_BLOCKS = 40
PIECE_ROWS = 48
SUB = 64
GROUP = 8
PRECISE = lax.Precision.HIGHEST
VMEM_BYTES = 56 * 2**20
Z_ORDER = (0, 1, 7, 2, 6, 3, 5, 4)
RING = (1, 3, 2)


def dot(a, b, dims=(((1,), (0,)), ((), ()))):
    return lax.dot_general(a, b, dims, precision=PRECISE, preferred_element_type=jnp.float32)


def interleave(parity):
    k = lax.broadcasted_iota(jnp.int32, (LANES, PIVOTS), 0)
    c = lax.broadcasted_iota(jnp.int32, (LANES, PIVOTS), 1)
    return (c == 2 * k + parity).astype(jnp.float32)


def factor_steps(d_ref, inv_ref):
    r = lax.broadcasted_iota(jnp.int32, (PIVOTS, PIVOTS), 0)
    c = lax.broadcasted_iota(jnp.int32, (PIVOTS, PIVOTS), 1)
    inv_ref[...] = (r == c).astype(jnp.float32)
    rs = lax.broadcasted_iota(jnp.int32, (SUB, SUB), 0)
    cs = lax.broadcasted_iota(jnp.int32, (SUB, SUB), 1)
    eye = (rs == cs).astype(jnp.float32)
    sub = lax.broadcasted_iota(jnp.int32, (GROUP, LANES), 0)
    for o in range(PIVOTS // SUB):
        lo, hi = o * SUB, (o + 1) * SUB
        rest = jnp.concatenate([d_ref[lo:hi, lo:hi], eye], 1)
        done = []
        for g in range(SUB // GROUP):
            height = SUB - g * GROUP
            below = lax.broadcasted_iota(jnp.int32, (height, LANES), 0)
            cols = [
                jnp.broadcast_to(rest[:, g * GROUP + k : g * GROUP + k + 1], (height, LANES)) for k in range(GROUP)
            ]
            scale = jnp.zeros((GROUP, LANES), jnp.float32)
            for j in range(GROUP):
                pivot = cols[j][j : j + 1]
                scale = jnp.where(sub == j, jnp.broadcast_to(pivot, (GROUP, LANES)), scale)
                factor = cols[j] * jnp.broadcast_to(1.0 / pivot, (height, LANES))
                factor = jnp.where(below > j, factor, 0.0)
                for k in range(j + 1, GROUP):
                    cols[k] = cols[k] - factor * jnp.broadcast_to(cols[k][j : j + 1], (height, LANES))
                rest = rest - factor * jnp.broadcast_to(rest[j : j + 1], (height, LANES))
            root = lax.rsqrt(scale)
            root = root * (1.5 - 0.5 * scale * root * root)
            done.append(rest[:GROUP] * root)
            rest = rest[GROUP:]
            yield
        small = jnp.concatenate(done, 0)[:, SUB:]
        top = dot(small, inv_ref[lo:hi, :])
        inv_ref[lo:hi, :] = top
        if hi < PIVOTS:
            lead = dot(small, d_ref[lo:hi, :])
            tail = lead[:, hi:]
            d_ref[hi:, :] = d_ref[hi:, :] - dot(tail, lead, (((0,), (0,)), ((), ())))
            inv_ref[hi:, :] = inv_ref[hi:, :] - dot(tail, top, (((0,), (0,)), ((), ())))
        yield


class Torus:
    def __init__(self, ny):
        self.me = lax.axis_index("cube")
        self.core = lax.axis_index("row")
        self.ny = ny
        self.z = self.me % NZ
        self.x = self.me // NZ % NX
        self.y = self.me // (NZ * NX)
        self.ly = self.y % ny
        self.base = self.y - self.ly
        self.ring_y = RING if ny == 4 else (1,)
        self.sibling = (1 - self.core, self.me)
        half = lax.axis_size("cube") // 2
        self.across = (self.core, (self.me + half) % (2 * half))
        self.started = []

    def chip(self, py, px, pz):
        return (self.core, (self.base + py) * (NX * NZ) + px * NZ + pz)

    def over_x(self, d):
        return self.chip(self.ly, (self.x + d) % NX, self.z)

    def over_y(self, d):
        return self.chip((self.ly + d) % self.ny, self.x, self.z)

    def over_z(self, d):
        return self.chip(self.ly, self.x, (self.z + d) % NZ)

    def peers(self):
        columns = [self.chip(self.ly, self.x, (self.z + d) % NZ) for d in range(1, NZ)]
        found = columns + [self.sibling]
        found += [self.over_x(d) for d in RING]
        return found + [(self.core, (self.y + d) % 4 * (NX * NZ) + self.x * NZ + self.z) for d in RING]

    def send(self, src, dst, ssem, rsem, peer):
        copy = pltpu.make_async_remote_copy(
            src_ref=src, dst_ref=dst, send_sem=ssem, recv_sem=rsem, device_id=peer, device_id_type=MESH
        )
        copy.start()
        self.started.append(copy)
        return copy


def gather_and_factor(at, first, second, pivots, inv_ref, d_ref, mine, theirs, own_ref, diag, sems, meanwhile):
    z_send, z_recv, p_send, p_recv, s_send, s_recv, t_send, t_recv = sems
    ny, x, z, ly = at.ny, at.x, at.z, at.ly
    over_x, over_y, over_z = at.over_x, at.over_y, at.over_z

    def small(stage, k, part, peer):
        return at.send(part, part, t_send.at[stage, k], t_recv.at[stage, k], peer)

    own = pivots.at[:, ly, x, z]
    tile = diag.at[at.core, ly, x, z]
    small_z = [small(0, d, tile, over_z(d)) for d in Z_ORDER[1:]]
    z_copies = {d: at.send(own, own, z_send.at[d], z_recv.at[d], over_z(d)) for d in Z_ORDER[1:]}
    blocks = at.send(mine, theirs, s_send, s_recv, at.sibling)
    hops = {}
    thirds = {}
    last = []

    def z_slice(t):
        return (z + NZ - Z_ORDER[t]) % NZ

    def view(part, py, px, t):
        return pivots.at[part[0], py, px, z_slice(t), part[1]]

    def piece(kind, t, k, part, peer):
        return at.send(part, part, p_send.at[kind, t, k], p_recv.at[kind, t, k], peer)

    def hop(t):
        if t:
            z_copies[Z_ORDER[t]].wait_recv()
        hops[t] = [piece(0, t, k, view(first, ly, x, t), over_x(d)) for k, d in enumerate(RING)]
        hops[t] += [piece(1, t, k, view(second, ly, x, t), over_y(d)) for k, d in enumerate(at.ring_y)]

    def third(t):
        for copy in hops[t]:
            copy.wait_recv()
        ways = (1, 3) if ny == 4 else at.ring_y
        thirds[t] = (
            [piece(2, t, k, view(first, ly, pl.ds(0, NX), t), over_y(d)) for k, d in enumerate(ways)],
            [piece(3, t, k, view(second, pl.ds(0, ny), x, t), over_x(d)) for k, d in enumerate((1, 3))],
        )

    def forward(t):
        over_ys, over_xs = thirds[t]
        if ny == 4:
            for k, d in enumerate((1, 3)):
                over_ys[k].wait_recv()
                last.append(piece(4, t, k, view(first, (ly + 4 - d) % 4, pl.ds(2 * k, 2), t), over_y(d)))
        else:
            last.extend(over_ys)
        for k, d in enumerate((1, 3)):
            over_xs[k].wait_recv()
            part = view(second, pl.ds(k * (ny // 2), ny // 2), (x + 4 - d) % 4, t)
            last.append(piece(5, t, k, part, over_x(d)))

    for copy in small_z:
        copy.wait_recv()
    small_x = [small(1, d, diag.at[at.core, ly, x], over_x(d)) for d in RING]
    hop(0)
    hop(1)
    hop(2)
    hop(3)
    hop(4)
    for copy in small_x:
        copy.wait_recv()
    small_y = [small(2, d, diag.at[at.core, ly], over_y(d)) for d in at.ring_y]
    hop(5)
    third(0)
    hop(6)
    third(1)
    third(2)
    hop(7)
    third(3)
    third(4)
    for copy in small_y:
        copy.wait_recv()
    small_core = small(3, 0, diag.at[at.core], at.sibling)
    meanwhile()
    d_ref[...] = dot(in_order(diag, at.core), interleave(at.core))
    blocks.wait_recv()
    own_ref[...] = dot(mine[...], interleave(at.core)) + dot(theirs[...], interleave(1 - at.core))
    small_core.wait_recv()
    d_ref[...] = d_ref[...] + dot(in_order(diag, 1 - at.core), interleave(1 - at.core))
    moves = {0: ((third, 5), (forward, 0)), 2: ((third, 6), (forward, 1)), 4: ((third, 7), (forward, 2))}
    moves.update({7 + 4 * t: ((forward, 3 + t),) for t in range(5)})
    for count, _ in enumerate(factor_steps(d_ref, inv_ref)):
        for move, t in moves.pop(count, ()):
            move(t)
    for group in moves.values():
        for move, t in group:
            move(t)

    def finish():
        for copy in last:
            copy.wait_recv()

    return finish


def in_order(diag, core):
    return jnp.concatenate([diag[core, :, :, :, i, :].reshape(-1, LANES) for i in range(diag.shape[4])], 0)


def solve_own(own, inv):
    return dot(dot(own, inv, (((1,), (1,)), ((), ()))), inv)


def split(a):
    high = a.astype(jnp.bfloat16)
    return high, (a - high.astype(jnp.float32)).astype(jnp.bfloat16)


def product(left, right):
    mul = functools.partial(jnp.dot, preferred_element_type=jnp.float32)
    (high, low), (top, rest) = left, right
    return mul(high, top) + (mul(high, rest) + mul(low, top))


def left_side(at, slots, pivot_slots, inv_ref, own_ref, sides, high_ref, low_ref):
    members = at.ny * NX * NZ
    inv = inv_ref[...]
    top = [-solve_own(own_ref[...], inv)] + sides
    rows = [inv_ref[pl.ds(i * members + at.me % members, 1), :] for i in range(pivot_slots)]
    rows += [jnp.zeros((high_ref.shape[0] - slots - pivot_slots, PIVOTS), jnp.float32)]
    below = jnp.concatenate(rows, 0)
    if sides:
        wide = sum(side.shape[1] for side in sides)
        below = jnp.concatenate([below, jnp.zeros((below.shape[0], wide), jnp.float32)], 1)
        top = [jnp.concatenate(top, 1)]
    high_ref[...], low_ref[...] = split(jnp.concatenate(top + [below], 0))


def along_lanes(map_ref, child, shape, per):
    lane = lax.broadcasted_iota(jnp.int32, shape, 1)
    found = jnp.full(shape, -1, jnp.int32)
    for u in range(UPDATE_BLOCKS):
        inside = lane == u + 1 if per == 1 else (lane == 2 * u) | (lane == 2 * u + 1)
        found = jnp.where(inside, map_ref[child, u], found)
    return found


def column_selector(map_ref, child):
    shape = (ROOT_BLOCKS, UPDATE_BLOCKS + 1)
    return (lax.broadcasted_iota(jnp.int32, shape, 0) == along_lanes(map_ref, child, shape, 1)).astype(jnp.float32)


def row_selector(map_ref, child):
    shape = (2 * ROOT_BLOCKS, PIECE_ROWS)
    row = lax.broadcasted_iota(jnp.int32, shape, 0)
    lane = lax.broadcasted_iota(jnp.int32, shape, 1)
    found = along_lanes(map_ref, child, shape, 2)
    return ((found >= 0) & (row == 2 * found + (lane & 1))).astype(jnp.float32)


def kernel(
    place_ref, map_ref, child_ref, root_ref, rest_ref, root_factor_ref, child_factor_ref,
    inv_ref, d_ref, few_own, few_other, held, leave, other, update,
    c_front, c_pivots, c_mine, c_theirs, c_own, c_diag, c_high, c_low,
    r_front, r_pivots, r_mine, r_theirs, r_own, r_diag, r_high, r_low,
    local_sem, *sems,
):
    c_sems, r_sems, (x_send, x_recv) = sems[:8], sems[8:16], sems[16:]
    at = Torus(2)
    slots, groups = child_ref.shape[0], child_ref.shape[1]
    pivot_slots = child_factor_ref.shape[0]
    whole = pltpu.make_async_copy(child_ref, c_front, local_sem.at[0])
    whole.start()
    local = pltpu.make_async_copy(child_ref.at[pl.ds(0, pivot_slots)], c_pivots.at[:, at.ly, at.x, at.z], local_sem.at[1])
    local.start()
    barrier = pltpu.get_barrier_semaphore()
    peers = at.peers()
    for peer in peers:
        pl.semaphore_signal(barrier, inc=1, device_id=peer, device_id_type=MESH)
    root_whole = pltpu.make_async_copy(root_ref, r_front, local_sem.at[2])
    root_whole.start()
    own_child = at.me // (lax.axis_size("cube") // 2)
    nothing = jnp.zeros((PIECE_ROWS, LANES), jnp.float32)
    held[0] = nothing
    leave[0] = nothing
    row_own, row_other = row_selector(map_ref, own_child), row_selector(map_ref, 1 - own_child)
    col_own, col_other = column_selector(map_ref, own_child), column_selector(map_ref, 1 - own_child)
    whole.wait()
    c_mine[...] = c_front[:, 0, :]
    c_diag[at.core, at.ly, at.x, at.z] = c_front[0:pivot_slots, 0, :]
    local.wait()
    pl.semaphore_wait(barrier, len(peers))

    all_groups = pl.ds(0, groups)
    halves = ((pl.ds(0, 2), all_groups), (pl.ds(2, 2), all_groups))
    finish = gather_and_factor(at, *halves, c_pivots, inv_ref, d_ref, c_mine, c_theirs, c_own, c_diag, c_sems, lambda: None)
    left_side(at, slots, pivot_slots, inv_ref, c_own, [], c_high, c_low)
    left = (c_high[...], c_low[...])
    finish()
    count = (slots - pivot_slots) // 2
    fill = nothing[: PIECE_ROWS - count]
    for k in range(0, groups, 2):
        pair = [c_pivots[:, :, :, :, k + e, :].reshape(PIVOTS, LANES) for e in range(2)]
        total = product(left, split(jnp.concatenate(pair, 1)))
        for e in range(2):
            part = total[:, e * LANES : (e + 1) * LANES]
            child_factor_ref[:, k + e, :] = part[slots : slots + pivot_slots]
            if k + e:
                update[k + e] = c_front[:, k + e, :] + part[:slots]
                even = update[k + e, pl.ds(pivot_slots, count, 2), :]
                odd = update[k + e, pl.ds(pivot_slots + 1, count, 2), :]
                held[k + e] = jnp.concatenate([jnp.where(own_child == 0, even, odd), fill], 0)
                leave[k + e] = jnp.concatenate([jnp.where(own_child == 0, odd, even), fill], 0)

    sent = at.started
    at = Torus(4)
    lead = jnp.maximum(place_ref[own_child, 0], 1)
    blocks = UPDATE_BLOCKS + 1
    for s in range(2):
        few_own[s, 0:blocks] = leave[:, pl.ds(2 * lead - 2 + s, 1), :].reshape(blocks, LANES)
    few_own[2] = leave[lead]
    few = at.send(few_own, few_other, x_send.at[0], x_recv.at[0], at.across)
    root_whole.wait()
    slots, groups = root_ref.shape[0], root_ref.shape[1]
    pivot_slots = root_factor_ref.shape[0]
    lines = []
    for s in range(pivot_slots):
        line = held[:, pl.ds(2 * lead - 2 + s, 1), :].reshape(blocks, LANES)
        lines.append(r_front[s, :, :] + dot(col_own, line))
    column = r_front[:, 0, :] + dot(row_own, held[lead])
    few.wait_recv()
    for s in range(pivot_slots):
        line = lines[s] + dot(col_other, few_other[s, 0:blocks])
        r_pivots[s, at.ly, at.x, at.z] = line
        r_diag[at.core, at.ly, at.x, at.z, s : s + 1, :] = line[0:1]
    r_mine[...] = column + dot(row_other, few_other[2])
    bulk = []

    def exchange():
        bulk.append(at.send(leave, other, x_send.at[1], x_recv.at[1], at.across))

    all_slots = pl.ds(0, pivot_slots)
    halves = ((all_slots, pl.ds(0, 8)), (all_slots, pl.ds(8, groups - 8)))
    finish = gather_and_factor(at, *halves, r_pivots, inv_ref, d_ref, r_mine, r_theirs, r_own, r_diag, r_sems, exchange)
    left_side(at, slots, pivot_slots, inv_ref, r_own, [row_own, row_other], r_high, r_low)
    left = (r_high[...], r_low[...])
    bulk[0].wait_recv()
    finish()
    for k in range(0, groups, 2):
        pair = []
        for n in (k, k + 1):
            pivots = r_pivots[:, :, :, :, n, :].reshape(PIVOTS, LANES)
            kept, arrived = held[place_ref[own_child, n]], other[place_ref[1 - own_child, n]]
            pair.append(jnp.concatenate([pivots, kept, arrived], 0))
        total = product(left, split(jnp.concatenate(pair, 1)))
        for e in range(2):
            part = total[:, e * LANES : (e + 1) * LANES]
            root_factor_ref[:, k + e, :] = part[slots : slots + pivot_slots]
            if k + e:
                rest = r_front[:, k + e, :] + part[:slots]
                rest_ref[:, 0, pl.ds((k + e - 1) * LANES, LANES)] = rest[pivot_slots:]
    for copy in sent + at.started:
        copy.wait_send()


def buffers(front, slots, ny, depth):
    rows, groups, lanes = front.shape
    f32 = jnp.float32
    height = -(-(rows + slots) // 16) * 16
    return [
        pltpu.VMEM((rows, groups, lanes), f32),
        pltpu.VMEM((slots, ny, NX, NZ, groups, lanes), f32),
        pltpu.VMEM((rows, lanes), f32),
        pltpu.VMEM((rows, lanes), f32),
        pltpu.VMEM((rows, PIVOTS), f32),
        pltpu.VMEM((2, ny, NX, NZ, slots, lanes), f32),
        pltpu.VMEM((height, depth), jnp.bfloat16),
        pltpu.VMEM((height, depth), jnp.bfloat16),
    ]


def semaphores():
    dma = pltpu.SemaphoreType.DMA
    return [dma((NZ,)), dma((NZ,)), dma((6, NZ, 3)), dma((6, NZ, 3)), dma, dma, dma((4, NZ)), dma((4, NZ))]


def eliminate(place, child_map, child, root):
    f32 = jnp.float32
    lanes = LANES
    dma = pltpu.SemaphoreType.DMA
    anywhere = pl.BlockSpec(memory_space=pl.ANY)
    in_vmem = pl.BlockSpec(memory_space=pltpu.VMEM)
    in_smem = pl.BlockSpec(memory_space=pltpu.SMEM)
    child_slots, root_slots = 4, 2
    few = pltpu.VMEM((3, PIECE_ROWS, lanes), f32)
    piece = pltpu.VMEM((UPDATE_BLOCKS + 1, PIECE_ROWS, lanes), f32)
    return pl.pallas_call(
        kernel,
        out_shape=(
            jax.ShapeDtypeStruct((root.shape[0] - root_slots, 1, (root.shape[1] - 1) * lanes), f32),
            jax.ShapeDtypeStruct((root_slots, root.shape[1], lanes), f32),
            jax.ShapeDtypeStruct((child_slots, child.shape[1], lanes), f32),
        ),
        in_specs=[in_smem, in_smem, anywhere, anywhere],
        out_specs=(in_vmem, in_vmem, in_vmem),
        scratch_shapes=[
            pltpu.VMEM((PIVOTS, PIVOTS), f32), pltpu.VMEM((PIVOTS, PIVOTS), f32), few, few, piece, piece, piece,
            pltpu.VMEM((child.shape[1], child.shape[0], lanes), f32),
            *buffers(child, child_slots, 2, PIVOTS), *buffers(root, root_slots, 4, PIVOTS + 2 * PIECE_ROWS),
            dma((3,)), *semaphores(), *semaphores(), dma((2,)), dma((2,)),
        ],
        compiler_params=pltpu.CompilerParams(
            collective_id=1, has_side_effects=True, vmem_limit_bytes=VMEM_BYTES
        ),
        name="eliminate_fronts",
    )(place, child_map, child, root)


def shards(child_fronts, root_front, child_map):
    child = child_fronts.reshape(child_fronts.shape[1], -1, LANES)
    root = root_front.reshape(root_front.shape[1], -1, LANES)
    blocks = jnp.arange(ROOT_BLOCKS, dtype=jnp.int32)[None, :, None]
    order = jnp.arange(1, UPDATE_BLOCKS + 1, dtype=jnp.int32)
    place = jnp.max(jnp.where(blocks == child_map[:, None, :], order, 0), 2)
    root_rest, root_factor, child_factor = eliminate(place, child_map, child, root)
    return (
        child_factor.reshape(1, 4, 1, -1),
        root_factor.reshape(1, 2, 1, -1),
        root_rest.reshape(1, 78, 1, -1),
    )


def solution(mesh):
    placed = P("cube", None, "row", None)
    return jax.shard_map(
        shards, mesh=mesh, in_specs=(placed, placed, P()), out_specs=(placed, placed, placed), check_vma=False
    )
```
